512 devices in a mesh: ia: 8 (over z_lo, core), ja: 16 (over z_hi, y), ka: 4 (over x).
Axes of the slice: x: 4, y: 4, z: 16 (z_hi: 4, z_lo: 4; z = z_hi * 4 + z_lo), core: 2. Of those that a mesh axis runs over, the one named last changes fastest.
Arguments:
- factor_a: bfloat16 [8, 2048, 128], P('ia', ('ja', 'ka')), may hold values from -6 to 6
- factor_b: bfloat16 [16, 1024, 128], P('ja', ('ia', 'ka')), may hold values from -6 to 6
- factor_c: bfloat16 [4, 4096, 128], P('ka', ('ia', 'ja')), may hold values from -6 to 6
- observed: bfloat16 [8, 16, 4, 36, 32, 1024], P('ia', 'ja', 'ka'), may hold values from -6 to 6
- coords: int32 [3, 8, 16, 4, 36], P(None, 'ia', 'ja', 'ka'), may hold values from 0 to 127, as said below
- counts: int32 [8, 16, 4], P('ia', 'ja', 'ka'), may hold values from 18 to 36, as said below
Outputs:
- residual: bfloat16 [8, 16, 4, 36, 32, 1024], P('ia', 'ja', 'ka')
- grad_a: float32 [8, 2048, 128], P('ia', ('ja', 'ka'))
- grad_b: float32 [16, 1024, 128], P('ja', ('ia', 'ka'))
- grad_c: float32 [4, 4096, 128], P('ka', ('ia', 'ja'))
The draws below stay inside these ranges and needn't reach their ends.
Inputs may be any that keep to these rules, and one draw needn't show every extreme that they name: `coords`: component 0 lies in 0 to 63, component 1 in 0 to 31, component 2 in 0 to 127; several slots may name the same block. Slots 0 to counts - 1 of a device are live; some device has all 36 slots live.
All inputs are finite; a program needn't handle non-finite values.
Results may differ from the reference program's by a relative error of at most 0.019.
Values may be sent and summed in bfloat16 or wider, within the bound.
No kernel may reach another device: no remote copies, remote signals or barrier semaphores. Data moves between devices by JAX's collectives and lax.ppermute only.
A program may use at most 64 MiB of HBM per device.

```python
import jax
import jax.numpy as jnp
from jax import lax

RANK = 128
BS = 32
NB = 36
SLAB_A = 2048
SLAB_B = 1024
SLAB_C = 4096
N_IA = 8
N_JA = 16
N_KA = 4


def draw_coords(key, part):
    key = jax.random.fold_in(key, 11)
    key_a, key_b, key_c = jax.random.split(key, 3)
    shape = (N_IA, N_JA, N_KA, NB)
    first = jax.random.randint(key_a, shape, 0, SLAB_A // BS, dtype=jnp.int32)
    second = jax.random.randint(key_b, shape, 0, SLAB_B // BS, dtype=jnp.int32)
    third = jax.random.randint(key_c, shape, 0, SLAB_C // BS, dtype=jnp.int32)
    return jnp.stack([first, second, third], axis=0)


def draw_counts(key, part):
    key = jax.random.fold_in(key, 23)
    key_load, key_pick = jax.random.split(key, 2)
    shape = (N_IA, N_JA, N_KA)
    loads = jax.random.randint(key_load, shape, NB // 2, NB + 1, dtype=jnp.int32)
    chosen = jax.random.randint(key_pick, (), 0, N_IA * N_JA * N_KA, dtype=jnp.int32)
    flat = jnp.arange(N_IA * N_JA * N_KA, dtype=jnp.int32).reshape(shape)
    return jnp.where(flat == chosen, NB, loads).astype(jnp.int32)


def shard_levels(key, shape, cuts, smallest, largest):
    loudness = 1.0
    for dim, parts in cuts:
        steps = jax.random.uniform(jax.random.fold_in(jax.random.fold_in(key, 6), dim), (parts,), jnp.float32, smallest / len(cuts), largest / len(cuts))
        loudness = loudness * jnp.repeat(jnp.exp(steps), shape[dim] // parts).reshape((-1,) + (1,) * (len(shape) - 1 - dim))
    return loudness


def normal_values(key, dims, deviation, most, cuts=(), held_as=jnp.bfloat16):
    entries = deviation * jax.random.normal(key, dims, jnp.float32)
    if cuts:
        entries = entries * shard_levels(key, dims, cuts, -0.22, 0.18)
    return jnp.clip(entries, -most, most).astype(held_as)


def setup_inputs(seed: int = 0) -> dict:
    seeds = jax.random.split(jax.random.key(seed), 7)
    factor_a = normal_values(seeds[0], (N_IA, SLAB_A, RANK), 0.45, 6.0, ((0, 8), (1, 64)))
    factor_b = normal_values(seeds[1], (N_JA, SLAB_B, RANK), 0.45, 6.0, ((0, 16), (1, 32)))
    factor_c = normal_values(seeds[2], (N_KA, SLAB_C, RANK), 0.45, 6.0, ((0, 4), (1, 128)))
    observed = normal_values(seeds[3], (N_IA, N_JA, N_KA, NB, BS, BS * BS), 1.0, 6.0, ((0, 8), (1, 16), (2, 4)))
    coords = draw_coords(jax.random.fold_in(seeds[6], 71), 0)
    counts = draw_counts(jax.random.fold_in(seeds[6], 71), 0)
    return {"factor_a": factor_a, "factor_b": factor_b, "factor_c": factor_c, "observed": observed, "coords": coords, "counts": counts}


def block_terms(tile_a, tile_b, tile_c, observed_blocks, weight):
    flt = jnp.float32
    groups, extent, columns = tile_a.shape
    pair_bc = (tile_b[:, :, None, :].astype(flt) * tile_c[:, None, :, :].astype(flt)).astype(jnp.bfloat16).astype(flt)
    pair_ac = (tile_a[:, :, None, :].astype(flt) * tile_c[:, None, :, :].astype(flt)).astype(jnp.bfloat16).astype(flt)
    pair_ab = (tile_a[:, :, None, :].astype(flt) * tile_b[:, None, :, :].astype(flt)).astype(jnp.bfloat16).astype(flt)
    model = jnp.einsum('gar,gbcr->gabc', tile_a.astype(flt), pair_bc, precision=lax.Precision.HIGHEST)
    cube_data = observed_blocks.reshape(groups, extent, extent, extent).astype(flt)
    resid = (weight[:, None, None, None] * (model - cube_data)).astype(jnp.bfloat16)
    resid_wide = resid.astype(flt)
    term_a = jnp.einsum('gabc,gbcr->gar', resid_wide, pair_bc, precision=lax.Precision.HIGHEST)
    term_b = jnp.einsum('gabc,gacr->gbr', resid_wide, pair_ac, precision=lax.Precision.HIGHEST)
    term_c = jnp.einsum('gabc,gabr->gcr', resid_wide, pair_ab, precision=lax.Precision.HIGHEST)
    return resid.reshape(groups, extent, extent * extent), term_a, term_b, term_c


def spread(index, terms, count):
    onehot = (index[:, None] == jnp.arange(count, dtype=jnp.int32)[None, :]).astype(jnp.float32)
    return jnp.einsum('gs,gar->sar', onehot, terms, precision=lax.Precision.HIGHEST)


def reference(factor_a, factor_b, factor_c, observed, coords, counts):
    count_a = SLAB_A // BS
    count_b = SLAB_B // BS
    count_c = SLAB_C // BS
    tiles_a = factor_a.reshape(N_IA, count_a, BS, RANK)
    tiles_b = factor_b.reshape(N_JA, count_b, BS, RANK)
    tiles_c = factor_c.reshape(N_KA, count_c, BS, RANK)
    init = (jnp.zeros((N_IA, count_a, BS, RANK), jnp.float32),
            jnp.zeros((N_JA, count_b, BS, RANK), jnp.float32),
            jnp.zeros((N_KA, count_c, BS, RANK), jnp.float32))

    def device_step(carry, flat):
        acc_a, acc_b, acc_c = carry
        first = (flat // (N_JA * N_KA)).astype(jnp.int32)
        second = ((flat // N_KA) % N_JA).astype(jnp.int32)
        third = (flat % N_KA).astype(jnp.int32)
        where_a = coords[0][first, second, third]
        where_b = coords[1][first, second, third]
        where_c = coords[2][first, second, third]
        tile_a = tiles_a[first][where_a]
        tile_b = tiles_b[second][where_b]
        tile_c = tiles_c[third][where_c]
        weight = (jnp.arange(NB, dtype=jnp.int32) < counts[first, second, third]).astype(jnp.float32)
        resid, term_a, term_b, term_c = block_terms(tile_a, tile_b, tile_c, observed[first, second, third], weight)
        acc_a = acc_a.at[first].add(spread(where_a, term_a, count_a))
        acc_b = acc_b.at[second].add(spread(where_b, term_b, count_b))
        acc_c = acc_c.at[third].add(spread(where_c, term_c, count_c))
        return (acc_a, acc_b, acc_c), resid

    flats = jnp.arange(N_IA * N_JA * N_KA, dtype=jnp.int32)
    (acc_a, acc_b, acc_c), resids = lax.scan(device_step, init, flats)
    scale = 1.0 / BS
    residual = resids.reshape(N_IA, N_JA, N_KA, NB, BS, BS * BS)
    grad_a = (acc_a * scale).reshape(N_IA, SLAB_A, RANK)
    grad_b = (acc_b * scale).reshape(N_JA, SLAB_B, RANK)
    grad_c = (acc_c * scale).reshape(N_KA, SLAB_C, RANK)
    return residual, grad_a, grad_b, grad_c
```

```python
import jax
import jax.numpy as jnp
from jax import lax
from jax.experimental import pallas as pl
from jax.experimental.pallas import tpu as pltpu
from jax.sharding import Mesh, PartitionSpec as P

BF = jnp.bfloat16
F32 = jnp.float32
T = 32
R = 128
UNROLL = 4

AB = 768
CY = 640


def cp_kernel(off, ab, c_own, c_oth, obs, res, out_ab, out_own, out_oth, acc_ab, acc_c):
    slots = obs.shape[0]
    acc_ab[...] = jnp.zeros_like(acc_ab)
    acc_c[...] = jnp.zeros_like(acc_c)
    count = off[5, 0]

    def at(row, s):
        return pl.ds(pl.multiple_of(off[row, s], T), T)

    def terms(s):
        ta = ab[at(0, s), :]
        tb = ab[at(1, s), :].astype(F32)
        where_c = at(2, s)
        tc = jnp.where(off[4, s] == 0, c_own[where_c, :].astype(F32), c_oth[where_c, :].astype(F32))
        pair = (tb[:, None, :] * tc[None, :, :]).reshape(T * T, R).astype(BF)
        model = lax.dot_general(ta, pair, (((1,), (1,)), ((), ())), preferred_element_type=F32)
        live = (s < count).astype(F32)
        resid = (live * (model - obs[s].astype(F32))).astype(BF)
        res[s] = resid
        term_a = jnp.dot(resid, pair, preferred_element_type=F32)
        wide = lax.dot_general(resid, ta, (((0,), (0,)), ((), ())), preferred_element_type=F32)
        wide = wide.reshape(T, T, R)
        term_b = jnp.sum(wide * tc[None, :, :], axis=1)
        term_c = jnp.sum(wide * tb[:, None, :], axis=0)
        return term_a, term_b, term_c

    def group(g, carry):
        base = g * UNROLL

        @pl.when(base < count)
        def _():
            found = [terms(base + u) for u in range(UNROLL)]
            for u, (term_a, term_b, term_c) in enumerate(found):
                s = base + u
                acc_ab[at(0, s), :] += term_a
                acc_ab[at(1, s), :] += term_b
                acc_c[at(3, s), :] += term_c

        @pl.when(base >= count)
        def _():
            res[pl.ds(base, UNROLL)] = jnp.zeros((UNROLL,) + res.shape[1:], BF)

        return carry

    lax.fori_loop(0, slots // UNROLL, group, 0)
    scale = 1.0 / T
    half = out_own.shape[0]
    out_ab[...] = (acc_ab[...] * scale).astype(BF)
    out_own[...] = acc_c[:half, :] * scale
    out_oth[...] = (acc_c[half:, :] * scale).astype(BF)


def run_kernel(off, ab, c_own, c_oth, obs):
    slots = obs.shape[0]
    vmem = pl.BlockSpec(memory_space=pltpu.VMEM)
    half = 4 * 512
    return pl.pallas_call(
        cp_kernel,
        out_shape=(
            jax.ShapeDtypeStruct((slots, T, T * T), BF),
            jax.ShapeDtypeStruct((4 * AB, R), BF),
            jax.ShapeDtypeStruct((half, R), F32),
            jax.ShapeDtypeStruct((half, R), BF),
        ),
        in_specs=[pl.BlockSpec(memory_space=pltpu.SMEM), vmem, vmem, vmem, vmem],
        out_specs=(vmem, vmem, vmem, vmem),
        scratch_shapes=[pltpu.VMEM((4 * AB, R), F32), pltpu.VMEM((2 * half, R), F32)],
        compiler_params=pltpu.CompilerParams(vmem_limit_bytes=40 * 1024 * 1024),
        cost_estimate=pl.CostEstimate(
            flops=slots * 8 * T * T * T * R, bytes_accessed=12_000_000, transcendentals=0
        ),
    )(off, ab, c_own, c_oth, obs)


def on_device(factor_a, factor_b, factor_c, observed, coords, counts):
    slots = observed.shape[3]
    fa, fb, fc = factor_a[0], factor_b[0], factor_c[0]
    zl, co, zh = lax.axis_index("zl"), lax.axis_index("co"), lax.axis_index("zh")
    same_zl = (jnp.arange(4) == zl)[:, None, None]
    swap = [(0, 1), (1, 0)]

    pa, pb, pc = coords[0].reshape(slots), coords[1].reshape(slots), coords[2].reshape(slots)
    off_a = (pa % 4) * AB + (pa // 4 % 4) * 128 + (pa // 16) * T
    off_b = (pb % 4) * AB + 512 + ((pb // 4 % 2) ^ co) * 128 + (pb // 8) * T
    c_y, c_zh, c_rel, c_zl = pc % 4, pc // 4 % 4, (pc // 16 % 2) ^ co, pc // 32
    in_plane = (c_zl * 4 + c_zh) * T
    off_c = c_y * CY + in_plane
    off_acc = c_rel * 2048 + c_y * 512 + in_plane
    live = jnp.broadcast_to(counts.reshape(1), (slots,))
    off = jnp.stack([off_a, off_b, off_c, off_acc, c_rel, live]).astype(jnp.int32)

    second = jnp.where(same_zl[:, :, :, None], fa, fb)
    send = jnp.concatenate(
        [jnp.broadcast_to(fc, (4, 4, T, R)), jnp.broadcast_to(second, (4, 4, T, R))], axis=2
    )
    got = lax.all_to_all(send.reshape(16, 2 * T, R), ("zl", "zh"), 0, 0, tiled=True)
    got = got.reshape(4, 4, 2 * T, R)
    c_z = got[:, :, :T].reshape(16 * T, R)
    a_z = lax.dynamic_index_in_dim(got, zl, 0, keepdims=False)[:, T:].reshape(4 * T, R)
    b_z = lax.dynamic_index_in_dim(got, zh, 1, keepdims=False)[:, T:]
    b_z = jnp.where(same_zl, fb, b_z).reshape(4 * T, R)
    b_oth = lax.ppermute(b_z, "co", swap)
    by_y = lax.all_gather(jnp.concatenate([c_z, a_z]), "y", axis=0)
    c_oth = lax.ppermute(by_y, "co", swap)
    by_x = lax.all_gather(
        jnp.concatenate([by_y[:, 512:].reshape(512, R), b_z, b_oth]), "x", axis=0
    )

    res, sum_ab, sum_own, sum_oth = run_kernel(
        off,
        by_x.reshape(4 * AB, R),
        by_y.reshape(4 * CY, R),
        c_oth.reshape(4 * CY, R),
        observed[0, 0, 0],
    )

    c_in = lax.ppermute(sum_oth, "co", swap)
    ab_in = lax.all_to_all(sum_ab.reshape(4, AB, R), "x", 0, 0, tiled=True)
    ab = jnp.sum(ab_in.astype(F32), axis=0)
    c_sum = (sum_own + c_in.astype(F32)).astype(BF).reshape(4, 512, R)
    b_in = lax.ppermute(ab[640:].astype(BF), "co", swap)
    ca_in = lax.all_to_all(
        jnp.concatenate([c_sum, ab[:512].astype(BF).reshape(4, 128, R)], axis=1),
        "y", 0, 0, tiled=True,
    )
    ca = jnp.sum(ca_in.astype(F32), axis=0)
    b_sum = (ab[512:640] + b_in.astype(F32)).reshape(4, 1, T, R)
    a_sum = ca[512:].reshape(1, 4, T, R)
    second = jnp.where(same_zl[:, :, :, None], a_sum, b_sum).astype(BF)
    send = jnp.concatenate([ca[:512].astype(BF).reshape(4, 4, T, R), second], axis=2)
    got = lax.all_to_all(send.reshape(16, 2 * T, R), ("zl", "zh"), 0, 0, tiled=True)
    got = got.reshape(4, 4, 2 * T, R)
    grad_c = jnp.sum(got[:, :, :T].astype(F32), axis=(0, 1))
    grad_a = jnp.sum(
        lax.dynamic_index_in_dim(got, zl, 0, keepdims=False)[:, T:].astype(F32), axis=0
    )
    b_got = lax.dynamic_index_in_dim(got, zh, 1, keepdims=False)[:, T:].astype(F32)
    grad_b = jnp.sum(jnp.where(same_zl, b_sum[:, 0], b_got), axis=0)
    return (res.reshape(observed.shape), grad_a[None], grad_b[None], grad_c[None])


def solution(mesh):
    fine = Mesh(mesh.devices.reshape(4, 2, 4, 4, 4), ("zl", "co", "zh", "y", "x"))
    ia, ja = ("zl", "co"), ("zh", "y")
    return jax.shard_map(
        on_device,
        mesh=fine,
        in_specs=(
            P(ia, (*ja, "x"), None),
            P(ja, (*ia, "x"), None),
            P("x", (*ia, *ja), None),
            P(ia, ja, "x", None, None, None),
            P(None, ia, ja, "x", None),
            P(ia, ja, "x"),
        ),
        out_specs=(
            P(ia, ja, "x", None, None, None),
            P(ia, (*ja, "x"), None),
            P(ja, (*ia, "x"), None),
            P("x", (*ia, *ja), None),
        ),
        check_vma=False,
    )
```

```python
import jax
import jax.numpy as jnp
from jax import lax
from jax.experimental import pallas as pl
from jax.experimental.pallas import tpu as pltpu
from jax.sharding import Mesh, PartitionSpec as P

BF = jnp.bfloat16
F32 = jnp.float32
T = 32
R = 128
UNROLL = 4
VMEM = pl.BlockSpec(memory_space=pltpu.VMEM)
SMEM = pl.BlockSpec(memory_space=pltpu.SMEM)
HBM = pl.BlockSpec(memory_space=pltpu.HBM)

AB = 768
CY = 640


def sds(rows, dtype=BF):
    return jax.ShapeDtypeStruct(rows + (R,) if isinstance(rows, tuple) else (rows, R), dtype)


def small(kernel, out_shape, *args):
    return pl.pallas_call(
        kernel,
        out_shape=out_shape,
        in_specs=[VMEM] * len(args),
        out_specs=jax.tree.map(lambda _: VMEM, out_shape),
        compiler_params=pltpu.CompilerParams(vmem_limit_bytes=8 * 1024 * 1024),
    )(*args)


def spread_kernel(fa, fb, fc, send, b_own, a_v, c_v, sem):
    zl = lax.axis_index("zl")
    copies = [
        pltpu.make_async_copy(src, dst, sem.at[n])
        for n, (src, dst) in enumerate(((fa, a_v), (fb, b_own), (fc, c_v)))
    ]
    for copy in copies:
        copy.start()
    for copy in copies:
        copy.wait()
    for i in range(4):
        second = jnp.where(zl == i, a_v[...], b_own[...])
        for j in range(4):
            send[4 * i + j, :T, :] = c_v[...]
            send[4 * i + j, T:, :] = second


def spread(fa, fb, fc):
    return pl.pallas_call(
        spread_kernel,
        out_shape=(sds((16, 2 * T)), sds(T)),
        in_specs=[HBM, HBM, HBM],
        out_specs=(VMEM, VMEM),
        scratch_shapes=[
            pltpu.VMEM((T, R), BF), pltpu.VMEM((T, R), BF), pltpu.SemaphoreType.DMA((3,))
        ],
        compiler_params=pltpu.CompilerParams(vmem_limit_bytes=60 * 1024 * 1024),
    )(fa, fb, fc)


def split_kernel(got, b_own, y_send, b_z):
    zl, zh = lax.axis_index("zl"), lax.axis_index("zh")
    for m in range(16):
        tile = got[m, :T, :]
        for k in range(4):
            y_send[k, m * T : (m + 1) * T, :] = tile
    for j in range(4):
        tile = got[4 * zl + j, T:, :]
        for k in range(4):
            y_send[k, 512 + j * T : 512 + (j + 1) * T, :] = tile
    for i in range(4):
        b_z[i * T : (i + 1) * T, :] = jnp.where(zl == i, b_own[...], got[4 * i + zh, T:, :])


def join_kernel(by_y, b_z, b_oth, x_send):
    for j in range(4):
        x_send[128 * j : 128 * (j + 1), :] = by_y[j, 512:, :]
    x_send[512:640, :] = b_z[...]
    x_send[640:, :] = b_oth[...]


def total(ref, rows):
    parts = [ref[k, rows, :].astype(F32) for k in range(4)]
    return (parts[0] + parts[1]) + (parts[2] + parts[3])


def pack_y_kernel(ab_in, own, c_in, y_send, b_own, b_oth):
    for k in range(4):
        rows = slice(512 * k, 512 * (k + 1))
        y_send[k, :512, :] = (own[rows, :] + c_in[rows, :].astype(F32)).astype(BF)
        y_send[k, 512:, :] = total(ab_in, slice(128 * k, 128 * (k + 1))).astype(BF)
    b_own[...] = total(ab_in, slice(512, 640))
    b_oth[...] = total(ab_in, slice(640, 768)).astype(BF)


def pack_z_kernel(ca_in, b_own, b_in, send, b_keep):
    zl = lax.axis_index("zl")
    for m in range(16):
        send[m, :T, :] = total(ca_in, slice(m * T, (m + 1) * T)).astype(BF)
    a = [total(ca_in, slice(512 + j * T, 512 + (j + 1) * T)) for j in range(4)]
    for i in range(4):
        rows = slice(i * T, (i + 1) * T)
        b = b_own[rows, :] + b_in[rows, :].astype(F32)
        for j in range(4):
            send[4 * i + j, T:, :] = jnp.where(zl == i, a[j], b).astype(BF)

        @pl.when(zl == i)
        def _():
            b_keep[...] = b


def last_kernel(got, b_keep, grad_a, grad_b, grad_c):
    zl, zh = lax.axis_index("zl"), lax.axis_index("zh")
    scale = 1.0 / T
    c = got[0, :T, :].astype(F32)
    for m in range(1, 16):
        c = c + got[m, :T, :].astype(F32)
    grad_c[...] = c * scale
    a = got[4 * zl, T:, :].astype(F32)
    for j in range(1, 4):
        a = a + got[4 * zl + j, T:, :].astype(F32)
    grad_a[...] = a * scale
    b = b_keep[...]
    for i in range(4):
        b = b + jnp.where(zl == i, 0.0, got[4 * i + zh, T:, :].astype(F32))
    grad_b[...] = b * scale


def cp_kernel(pos, counts, ab, own, oth, obs, res, out_ab, out_own, out_oth,
              acc_ab, acc, obs_v, res_v, in_sem, out_sem):
    slots = obs.shape[0]
    groups = slots // UNROLL
    co = lax.axis_index("co")
    count = counts[0]

    def load(g):
        part = pl.ds(g * UNROLL, UNROLL)
        return pltpu.make_async_copy(obs.at[part], obs_v.at[part], in_sem.at[g])

    def store(g):
        part = pl.ds(g * UNROLL, UNROLL)
        return pltpu.make_async_copy(res_v.at[part], res.at[part], out_sem.at[g])

    for g in range(groups):
        load(g).start()
    acc_ab[...] = jnp.zeros_like(acc_ab)
    acc[...] = jnp.zeros_like(acc)

    def rows(start):
        return pl.ds(pl.multiple_of(start, T), T)

    def places(s):
        pa, pb, pc = pos[0, s], pos[1, s], pos[2, s]
        at_a = (pa & 3) * AB + ((pa >> 2) & 3) * 128 + (pa >> 4) * T
        at_b = (pb & 3) * AB + 512 + (((pb >> 2) & 1) ^ co) * 128 + (pb >> 3) * T
        in_plane = ((pc >> 5) * 4 + ((pc >> 2) & 3)) * T
        return at_a, at_b, pc & 3, in_plane, ((pc >> 4) & 1) ^ co

    def terms(s):
        at_a, at_b, y, in_plane, other = places(s)
        ta = ab[rows(at_a), :]
        tb = ab[rows(at_b), :].astype(F32)
        at_c = rows(y * CY + in_plane)
        tc = jnp.where(other == 0, own[at_c, :].astype(F32), oth[at_c, :].astype(F32))
        pair = (tb[:, None, :] * tc[None, :, :]).reshape(T * T, R).astype(BF)
        model = lax.dot_general(ta, pair, (((1,), (1,)), ((), ())), preferred_element_type=F32)
        live = (s < count).astype(F32)
        resid = (live * (model - obs_v[s].astype(F32))).astype(BF)
        res_v[s] = resid
        term_a = jnp.dot(resid, pair, preferred_element_type=F32)
        wide = lax.dot_general(resid, ta, (((0,), (0,)), ((), ())), preferred_element_type=F32)
        wide = wide.reshape(T, T, R)
        term_b = jnp.sum(wide * tc[None, :, :], axis=1)
        term_c = jnp.sum(wide * tb[:, None, :], axis=0)
        return term_a, term_b, term_c

    def group(g, carry):
        base = g * UNROLL
        load(g).wait()

        @pl.when(base < count)
        def _():
            found = [terms(base + u) for u in range(UNROLL)]
            for u, (term_a, term_b, term_c) in enumerate(found):
                at_a, at_b, y, in_plane, other = places(base + u)
                acc_ab[rows(at_a), :] += term_a
                acc_ab[rows(at_b), :] += term_b
                acc[rows(other * 2048 + y * 512 + in_plane), :] += term_c

        @pl.when(base >= count)
        def _():
            res_v[pl.ds(base, UNROLL)] = jnp.zeros((UNROLL,) + res.shape[1:], BF)

        store(g).start()
        return carry

    lax.fori_loop(0, groups, group, 0)
    out_ab[...] = acc_ab[...].astype(BF)
    out_own[...] = acc[:2048, :]
    out_oth[...] = acc[2048:, :].astype(BF)
    for g in range(groups):
        store(g).wait()


def run_kernel(pos, counts, ab, own, oth, obs):
    slots = obs.shape[0]
    groups = slots // UNROLL
    return pl.pallas_call(
        cp_kernel,
        out_shape=(jax.ShapeDtypeStruct(obs.shape, BF),
                   sds(4 * AB), sds(2048, F32), sds(2048)),
        in_specs=[SMEM, SMEM, VMEM, VMEM, VMEM, HBM],
        out_specs=(HBM, VMEM, VMEM, VMEM),
        scratch_shapes=[
            pltpu.VMEM((4 * AB, R), F32),
            pltpu.VMEM((4096, R), F32),
            pltpu.VMEM(obs.shape, BF),
            pltpu.VMEM(obs.shape, BF),
            pltpu.SemaphoreType.DMA((groups,)),
            pltpu.SemaphoreType.DMA((groups,)),
        ],
        compiler_params=pltpu.CompilerParams(vmem_limit_bytes=48 * 1024 * 1024),
        cost_estimate=pl.CostEstimate(
            flops=slots * 8 * T * T * T * R, bytes_accessed=12_000_000, transcendentals=0
        ),
    )(pos, counts, ab, own, oth, obs)


def on_device(factor_a, factor_b, factor_c, observed, coords, counts):
    slots = observed.shape[3]
    fa, fb, fc = factor_a[0], factor_b[0], factor_c[0]
    swap = [(0, 1), (1, 0)]

    send, b_own = spread(fa, fb, fc)
    got = lax.all_to_all(send, ("zl", "zh"), 0, 0, tiled=True)
    y_send, b_z = small(split_kernel, (sds((4, CY)), sds(128)), got, b_own)
    by_y = lax.all_to_all(y_send, "y", 0, 0, tiled=True)
    b_oth = lax.ppermute(b_z, "co", swap)
    x_send = small(join_kernel, sds(AB), by_y, b_z, b_oth)
    by_y, x_send = lax.optimization_barrier((by_y, x_send))
    by_x = lax.all_gather(x_send, "x", axis=0)
    c_oth = lax.ppermute(by_y, "co", swap)

    res, sum_ab, sum_own, sum_oth = run_kernel(
        coords.reshape(3, slots),
        counts.reshape(1),
        by_x.reshape(4 * AB, R),
        by_y.reshape(4 * CY, R),
        c_oth.reshape(4 * CY, R),
        observed[0, 0, 0],
    )

    ab_in = lax.all_to_all(sum_ab.reshape(4, AB, R), "x", 0, 0, tiled=True)
    c_in = lax.ppermute(sum_oth, "co", swap)
    y_send, b_own, b_send = small(
        pack_y_kernel, (sds((4, CY)), sds(128, F32), sds(128)), ab_in, sum_own, c_in
    )
    ca_in = lax.all_to_all(y_send, "y", 0, 0, tiled=True)
    b_in = lax.ppermute(b_send, "co", swap)
    send, b_keep = small(
        pack_z_kernel, (sds((16, 2 * T)), sds(T, F32)), ca_in, b_own, b_in
    )
    got = lax.all_to_all(send, ("zl", "zh"), 0, 0, tiled=True)
    grad_a, grad_b, grad_c = small(last_kernel, (sds(T, F32),) * 3, got, b_keep)
    return (res.reshape(observed.shape), grad_a[None], grad_b[None], grad_c[None])


def solution(mesh):
    fine = Mesh(mesh.devices.reshape(4, 2, 4, 4, 4), ("zl", "co", "zh", "y", "x"))
    ia, ja = ("zl", "co"), ("zh", "y")
    return jax.shard_map(
        on_device,
        mesh=fine,
        in_specs=(
            P(ia, (*ja, "x"), None),
            P(ja, (*ia, "x"), None),
            P("x", (*ia, *ja), None),
            P(ia, ja, "x", None, None, None),
            P(None, ia, ja, "x", None),
            P(ia, ja, "x"),
        ),
        out_specs=(
            P(ia, ja, "x", None, None, None),
            P(ia, (*ja, "x"), None),
            P(ja, (*ia, "x"), None),
            P("x", (*ia, *ja), None),
        ),
        check_vma=False,
    )
```

```python
import jax
import jax.numpy as jnp
from jax import lax
from jax.experimental import pallas as pl
from jax.experimental.pallas import tpu as pltpu
from jax.sharding import Mesh, PartitionSpec as P

BF = jnp.bfloat16
F32 = jnp.float32
T = 32
R = 128
UNROLL = 12
VMEM = pl.BlockSpec(memory_space=pltpu.VMEM)
SMEM = pl.BlockSpec(memory_space=pltpu.SMEM)
HBM = pl.BlockSpec(memory_space=pltpu.HBM)

AB = 768
CY = 640


def sds(rows, dtype=BF):
    return jax.ShapeDtypeStruct(rows + (R,) if isinstance(rows, tuple) else (rows, R), dtype)


def small(kernel, out_shape, *args):
    return pl.pallas_call(
        kernel,
        out_shape=out_shape,
        in_specs=[VMEM] * len(args),
        out_specs=jax.tree.map(lambda _: VMEM, out_shape),
        compiler_params=pltpu.CompilerParams(vmem_limit_bytes=8 * 1024 * 1024),
    )(*args)


def spread_kernel(fa, fb, fc, send, a_v, b_v, c_v, sem):
    zl = lax.axis_index("zl")
    copies = [
        pltpu.make_async_copy(src, dst, sem.at[n])
        for n, (src, dst) in enumerate(((fa, a_v), (fb, b_v), (fc, c_v)))
    ]
    for copy in copies:
        copy.start()
    for copy in copies:
        copy.wait()
    for i in range(4):
        second = jnp.where(zl == i, a_v[...], b_v[...])
        for j in range(4):
            send[4 * j + i, :T, :] = c_v[...]
            send[4 * j + i, T:, :] = second


def spread(fa, fb, fc):
    return pl.pallas_call(
        spread_kernel,
        out_shape=sds((16, 2 * T)),
        in_specs=[HBM, HBM, HBM],
        out_specs=VMEM,
        scratch_shapes=[pltpu.VMEM((T, R), BF)] * 3 + [pltpu.SemaphoreType.DMA((3,))],
        compiler_params=pltpu.CompilerParams(vmem_limit_bytes=60 * 1024 * 1024),
    )(fa, fb, fc)


def split_kernel(got, fb, y_send, b_z, b_v, sem):
    own = pltpu.make_async_copy(fb, b_v, sem)
    own.start()
    zl, zh = lax.axis_index("zl"), lax.axis_index("zh")
    for m in range(16):
        tile = got[m, :T, :]
        for k in range(4):
            y_send[k, m * T : (m + 1) * T, :] = tile
    for j in range(4):
        tile = got[4 * j + zl, T:, :]
        for k in range(4):
            y_send[k, 512 + j * T : 512 + (j + 1) * T, :] = tile
    own.wait()
    for i in range(4):
        b_z[i * T : (i + 1) * T, :] = jnp.where(zl == i, b_v[...], got[4 * zh + i, T:, :])


def split(got, fb):
    return pl.pallas_call(
        split_kernel,
        out_shape=(sds((4, CY)), sds(128)),
        in_specs=[VMEM, HBM],
        out_specs=(VMEM, VMEM),
        scratch_shapes=[pltpu.VMEM((T, R), BF), pltpu.SemaphoreType.DMA],
        compiler_params=pltpu.CompilerParams(vmem_limit_bytes=48 * 1024 * 1024),
    )(got, fb)


def join_kernel(by_y, b_z, b_oth, x_send):
    for j in range(4):
        x_send[128 * j : 128 * (j + 1), :] = by_y[j, 512:, :]
    x_send[512:640, :] = b_z[...]
    x_send[640:, :] = b_oth[...]


def total(ref, rows):
    parts = [ref[k, rows, :].astype(F32) for k in range(4)]
    return (parts[0] + parts[1]) + (parts[2] + parts[3])


def pack_y_kernel(ab_in, own, c_in, y_send, b_own, b_oth):
    for k in range(4):
        rows = slice(512 * k, 512 * (k + 1))
        y_send[k, :512, :] = (own[rows, :] + c_in[rows, :].astype(F32)).astype(BF)
        y_send[k, 512:, :] = total(ab_in, slice(128 * k, 128 * (k + 1))).astype(BF)
    b_own[...] = total(ab_in, slice(512, 640))
    b_oth[...] = total(ab_in, slice(640, 768)).astype(BF)


def pack_z_kernel(ca_in, b_own, b_in, send, b_keep):
    zl = lax.axis_index("zl")
    for m in range(16):
        send[m, :T, :] = total(ca_in, slice(m * T, (m + 1) * T)).astype(BF)
    a = [total(ca_in, slice(512 + j * T, 512 + (j + 1) * T)) for j in range(4)]
    for i in range(4):
        rows = slice(i * T, (i + 1) * T)
        b = b_own[rows, :] + b_in[rows, :].astype(F32)
        for j in range(4):
            send[4 * j + i, T:, :] = jnp.where(zl == i, a[j], b).astype(BF)

        @pl.when(zl == i)
        def _():
            b_keep[...] = b


def last_kernel(got, b_keep, grad_a, grad_b, grad_c):
    zl, zh = lax.axis_index("zl"), lax.axis_index("zh")
    scale = 1.0 / T
    c = got[0, :T, :].astype(F32)
    for m in range(1, 16):
        c = c + got[m, :T, :].astype(F32)
    grad_c[...] = c * scale
    a = got[zl, T:, :].astype(F32)
    for j in range(1, 4):
        a = a + got[4 * j + zl, T:, :].astype(F32)
    grad_a[...] = a * scale
    b = b_keep[...]
    for i in range(4):
        b = b + jnp.where(zl == i, 0.0, got[4 * zh + i, T:, :].astype(F32))
    grad_b[...] = b * scale


def cp_kernel(pos, counts, ab, own, oth, obs, res, out_ab, out_own, out_oth,
              acc_ab, acc, obs_v, res_v, in_sem, out_sem):
    slots = obs.shape[0]
    groups = slots // UNROLL
    co = lax.axis_index("co")
    count = counts[0]

    def load(g):
        part = pl.ds(g * UNROLL, UNROLL)
        return pltpu.make_async_copy(obs.at[part], obs_v.at[part], in_sem.at[g])

    def store(g):
        part = pl.ds(g * UNROLL, UNROLL)
        return pltpu.make_async_copy(res_v.at[part], res.at[part], out_sem.at[g])

    for g in range(groups):
        load(g).start()
    acc_ab[...] = jnp.zeros_like(acc_ab)
    acc[...] = jnp.zeros_like(acc)

    def rows(start):
        return pl.ds(pl.multiple_of(start, T), T)

    def places(s):
        pa, pb, pc = pos[0, s], pos[1, s], pos[2, s]
        at_a = (pa & 3) * AB + ((pa >> 2) & 3) * 128 + (pa >> 4) * T
        at_b = (pb & 3) * AB + 512 + (((pb >> 2) & 1) ^ co) * 128 + (pb >> 3) * T
        in_plane = (((pc >> 2) & 3) * 4 + (pc >> 5)) * T
        return at_a, at_b, pc & 3, in_plane, ((pc >> 4) & 1) ^ co

    def tiles(s):
        at_a, at_b, y, in_plane, other = places(s)
        at_c = rows(y * CY + in_plane)
        tc = jnp.where(other == 0, own[at_c, :].astype(F32), oth[at_c, :].astype(F32))
        return ab[rows(at_a), :], ab[rows(at_b), :].astype(F32), tc

    def two(s):
        (ta0, tb0, tc0), (ta1, tb1, tc1) = tiles(s), tiles(s + 1)
        none = jnp.zeros((T, R), BF)
        ta = jnp.concatenate(
            [jnp.concatenate([ta0, none], axis=1), jnp.concatenate([none, ta1], axis=1)], axis=0
        )
        tb = jnp.concatenate([tb0, tb1], axis=1)
        tc = jnp.concatenate([tc0, tc1], axis=1)
        pair = (tb[:, None, :] * tc[None, :, :]).reshape(T * T, 2 * R).astype(BF)
        model = lax.dot_general(ta, pair, (((1,), (1,)), ((), ())), preferred_element_type=F32)
        resids = []
        for u in range(2):
            live = (s + u < count).astype(F32)
            part = live * (model[u * T : (u + 1) * T, :] - obs_v[s + u].astype(F32))
            resids.append(part.astype(BF))
            res_v[s + u] = resids[u]
        resid = jnp.concatenate(resids, axis=0)
        term_a = jnp.dot(resid, pair, preferred_element_type=F32)
        wide = lax.dot_general(resid, ta, (((0,), (0,)), ((), ())), preferred_element_type=F32)
        wide = wide.reshape(T, T, 2 * R)
        term_b = jnp.sum(wide * tc[None, :, :], axis=1)
        term_c = jnp.sum(wide * tb[:, None, :], axis=0)
        return [
            (term_a[u * T : (u + 1) * T, u * R : (u + 1) * R],
             term_b[:, u * R : (u + 1) * R], term_c[:, u * R : (u + 1) * R])
            for u in range(2)
        ]

    def group(g, carry):
        base = g * UNROLL
        load(g).wait()

        @pl.when(base < count)
        def _():
            found = [t for u in range(0, UNROLL, 2) for t in two(base + u)]
            for u, (term_a, term_b, term_c) in enumerate(found):
                at_a, at_b, y, in_plane, other = places(base + u)
                acc_ab[rows(at_a), :] += term_a
                acc_ab[rows(at_b), :] += term_b
                acc[rows(other * 2048 + y * 512 + in_plane), :] += term_c

        @pl.when(base >= count)
        def _():
            res_v[pl.ds(base, UNROLL)] = jnp.zeros((UNROLL,) + res.shape[1:], BF)

        store(g).start()
        return carry

    lax.fori_loop(0, groups, group, 0)
    out_ab[...] = acc_ab[...].astype(BF)
    out_own[...] = acc[:2048, :]
    out_oth[...] = acc[2048:, :].astype(BF)
    for g in range(groups):
        store(g).wait()


def run_kernel(pos, counts, ab, own, oth, obs):
    slots = obs.shape[0]
    groups = slots // UNROLL
    return pl.pallas_call(
        cp_kernel,
        out_shape=(jax.ShapeDtypeStruct(obs.shape, BF),
                   sds(4 * AB), sds(2048, F32), sds(2048)),
        in_specs=[SMEM, SMEM, VMEM, VMEM, VMEM, HBM],
        out_specs=(HBM, VMEM, VMEM, VMEM),
        scratch_shapes=[
            pltpu.VMEM((4 * AB, R), F32),
            pltpu.VMEM((4096, R), F32),
            pltpu.VMEM(obs.shape, BF),
            pltpu.VMEM(obs.shape, BF),
            pltpu.SemaphoreType.DMA((groups,)),
            pltpu.SemaphoreType.DMA((groups,)),
        ],
        compiler_params=pltpu.CompilerParams(vmem_limit_bytes=48 * 1024 * 1024),
        cost_estimate=pl.CostEstimate(
            flops=slots * 8 * T * T * T * R, bytes_accessed=12_000_000, transcendentals=0
        ),
    )(pos, counts, ab, own, oth, obs)


def on_device(factor_a, factor_b, factor_c, observed, coords, counts):
    slots = observed.shape[3]
    fa, fb, fc = factor_a[0], factor_b[0], factor_c[0]
    swap = [(0, 1), (1, 0)]

    send = spread(fa, fb, fc)
    got = lax.all_to_all(send, ("zh", "zl"), 0, 0, tiled=True)
    y_send, b_z = split(got, fb)
    by_y = lax.all_to_all(y_send, "y", 0, 0, tiled=True)
    b_oth = lax.ppermute(b_z, "co", swap)
    x_send = small(join_kernel, sds(AB), by_y, b_z, b_oth)
    by_y, x_send = lax.optimization_barrier((by_y, x_send))
    by_x = lax.all_gather(x_send, "x", axis=0)
    c_oth = lax.ppermute(by_y, "co", swap)

    res, sum_ab, sum_own, sum_oth = run_kernel(
        coords.reshape(3, slots),
        counts.reshape(1),
        by_x.reshape(4 * AB, R),
        by_y.reshape(4 * CY, R),
        c_oth.reshape(4 * CY, R),
        observed[0, 0, 0],
    )

    ab_in = lax.all_to_all(sum_ab.reshape(4, AB, R), "x", 0, 0, tiled=True)
    c_in = lax.ppermute(sum_oth, "co", swap)
    y_send, b_own, b_send = small(
        pack_y_kernel, (sds((4, CY)), sds(128, F32), sds(128)), ab_in, sum_own, c_in
    )
    ca_in = lax.all_to_all(y_send, "y", 0, 0, tiled=True)
    b_in = lax.ppermute(b_send, "co", swap)
    send, b_keep = small(
        pack_z_kernel, (sds((16, 2 * T)), sds(T, F32)), ca_in, b_own, b_in
    )
    got = lax.all_to_all(send, ("zh", "zl"), 0, 0, tiled=True)
    grad_a, grad_b, grad_c = small(last_kernel, (sds(T, F32),) * 3, got, b_keep)
    return (res.reshape(observed.shape), grad_a[None], grad_b[None], grad_c[None])


def solution(mesh):
    fine = Mesh(mesh.devices.reshape(4, 2, 4, 4, 4), ("zl", "co", "zh", "y", "x"))
    ia, ja = ("zl", "co"), ("zh", "y")
    return jax.shard_map(
        on_device,
        mesh=fine,
        in_specs=(
            P(ia, (*ja, "x"), None),
            P(ja, (*ia, "x"), None),
            P("x", (*ia, *ja), None),
            P(ia, ja, "x", None, None, None),
            P(None, ia, ja, "x", None),
            P(ia, ja, "x"),
        ),
        out_specs=(
            P(ia, ja, "x", None, None, None),
            P(ia, (*ja, "x"), None),
            P(ja, (*ia, "x"), None),
            P("x", (*ia, *ja), None),
        ),
        check_vma=False,
    )
```

```python
import jax
import jax.numpy as jnp
from jax import lax
from jax.experimental import pallas as pl
from jax.experimental.pallas import tpu as pltpu
from jax.sharding import Mesh, PartitionSpec as P

BF = jnp.bfloat16
F32 = jnp.float32
T = 32
R = 128
UNROLL = 36
VMEM = pl.BlockSpec(memory_space=pltpu.VMEM)
SMEM = pl.BlockSpec(memory_space=pltpu.SMEM)
HBM = pl.BlockSpec(memory_space=pltpu.HBM)

AB = 768
CY = 640


def sds(rows, dtype=BF):
    return jax.ShapeDtypeStruct(rows + (R,) if isinstance(rows, tuple) else (rows, R), dtype)


def small(kernel, out_shape, *args):
    return pl.pallas_call(
        kernel,
        out_shape=out_shape,
        in_specs=[VMEM] * len(args),
        out_specs=jax.tree.map(lambda _: VMEM, out_shape),
        compiler_params=pltpu.CompilerParams(vmem_limit_bytes=8 * 1024 * 1024),
    )(*args)


def spread_kernel(fa, fb, fc, send, a_v, b_v, c_v, sem):
    zl = lax.axis_index("zl")
    copies = [
        pltpu.make_async_copy(src, dst, sem.at[n])
        for n, (src, dst) in enumerate(((fa, a_v), (fb, b_v), (fc, c_v)))
    ]
    for copy in copies:
        copy.start()
    for copy in copies:
        copy.wait()
    for i in range(4):
        second = jnp.where(zl == i, a_v[...], b_v[...])
        for j in range(4):
            send[4 * j + i, :T, :] = c_v[...]
            send[4 * j + i, T:, :] = second


def spread(fa, fb, fc):
    return pl.pallas_call(
        spread_kernel,
        out_shape=sds((16, 2 * T)),
        in_specs=[HBM, HBM, HBM],
        out_specs=VMEM,
        scratch_shapes=[pltpu.VMEM((T, R), BF)] * 3 + [pltpu.SemaphoreType.DMA((3,))],
        compiler_params=pltpu.CompilerParams(vmem_limit_bytes=60 * 1024 * 1024),
    )(fa, fb, fc)


def fetch_kernel(fb, b_own, sem):
    copy = pltpu.make_async_copy(fb, b_own, sem)
    copy.start()
    copy.wait()


def fetch(fb):
    return pl.pallas_call(
        fetch_kernel,
        out_shape=sds(T),
        in_specs=[HBM],
        out_specs=VMEM,
        scratch_shapes=[pltpu.SemaphoreType.DMA],
        compiler_params=pltpu.CompilerParams(vmem_limit_bytes=8 * 1024 * 1024),
        cost_estimate=pl.CostEstimate(flops=0, bytes_accessed=1_000_000, transcendentals=0),
    )(fb)


def split_kernel(got, b_own, y_send, b_z):
    zl, zh = lax.axis_index("zl"), lax.axis_index("zh")
    for m in range(16):
        tile = got[m, :T, :]
        for k in range(4):
            y_send[k, m * T : (m + 1) * T, :] = tile
    for j in range(4):
        tile = got[4 * j + zl, T:, :]
        for k in range(4):
            y_send[k, 512 + j * T : 512 + (j + 1) * T, :] = tile
    for i in range(4):
        b_z[i * T : (i + 1) * T, :] = jnp.where(zl == i, b_own[...], got[4 * zh + i, T:, :])


def join_kernel(by_y, b_z, b_oth, x_send):
    for j in range(4):
        x_send[128 * j : 128 * (j + 1), :] = by_y[j, 512:, :]
    x_send[512:640, :] = b_z[...]
    x_send[640:, :] = b_oth[...]


def total(ref, rows):
    parts = [ref[k, rows, :].astype(F32) for k in range(4)]
    return (parts[0] + parts[1]) + (parts[2] + parts[3])


def pack_y_kernel(ab_in, own, c_in, y_send, b_own, b_oth):
    for k in range(4):
        rows = slice(512 * k, 512 * (k + 1))
        y_send[k, :512, :] = (own[rows, :] + c_in[rows, :].astype(F32)).astype(BF)
        y_send[k, 512:, :] = total(ab_in, slice(128 * k, 128 * (k + 1))).astype(BF)
    b_own[...] = total(ab_in, slice(512, 640))
    b_oth[...] = total(ab_in, slice(640, 768)).astype(BF)


def pack_z_kernel(ca_in, b_own, b_in, send, b_keep):
    zl = lax.axis_index("zl")
    for m in range(16):
        send[m, :T, :] = total(ca_in, slice(m * T, (m + 1) * T)).astype(BF)
    a = [total(ca_in, slice(512 + j * T, 512 + (j + 1) * T)) for j in range(4)]
    for i in range(4):
        rows = slice(i * T, (i + 1) * T)
        b = b_own[rows, :] + b_in[rows, :].astype(F32)
        for j in range(4):
            send[4 * j + i, T:, :] = jnp.where(zl == i, a[j], b).astype(BF)

        @pl.when(zl == i)
        def _():
            b_keep[...] = b


def last_kernel(got, b_keep, grad_a, grad_b, grad_c):
    zl, zh = lax.axis_index("zl"), lax.axis_index("zh")
    scale = 1.0 / T
    c = got[0, :T, :].astype(F32)
    for m in range(1, 16):
        c = c + got[m, :T, :].astype(F32)
    grad_c[...] = c * scale
    a = got[zl, T:, :].astype(F32)
    for j in range(1, 4):
        a = a + got[4 * j + zl, T:, :].astype(F32)
    grad_a[...] = a * scale
    b = b_keep[...]
    for i in range(4):
        b = b + jnp.where(zl == i, 0.0, got[4 * zh + i, T:, :].astype(F32))
    grad_b[...] = b * scale


def cp_kernel(pos, counts, ab, own, oth, obs, res, out_ab, out_own, out_oth,
              acc_ab, acc, obs_v, res_v, in_sem, out_sem):
    slots = obs.shape[0]
    groups = slots // UNROLL
    co = lax.axis_index("co")
    count = counts[0]

    def load(g):
        part = pl.ds(g * UNROLL, UNROLL)
        return pltpu.make_async_copy(obs.at[part], obs_v.at[part], in_sem.at[g])

    def store(g):
        part = pl.ds(g * UNROLL, UNROLL)
        return pltpu.make_async_copy(res_v.at[part], res.at[part], out_sem.at[g])

    for g in range(groups):
        load(g).start()
    acc_ab[...] = jnp.zeros_like(acc_ab)
    acc[...] = jnp.zeros_like(acc)

    def rows(start):
        return pl.ds(pl.multiple_of(start, T), T)

    def places(s):
        pa, pb, pc = pos[0, s], pos[1, s], pos[2, s]
        at_a = (pa & 3) * AB + ((pa >> 2) & 3) * 128 + (pa >> 4) * T
        at_b = (pb & 3) * AB + 512 + (((pb >> 2) & 1) ^ co) * 128 + (pb >> 3) * T
        in_plane = (((pc >> 2) & 3) * 4 + (pc >> 5)) * T
        return at_a, at_b, pc & 3, in_plane, ((pc >> 4) & 1) ^ co

    def tiles(s):
        at_a, at_b, y, in_plane, other = places(s)
        at_c = rows(y * CY + in_plane)
        tc = jnp.where(other == 0, own[at_c, :].astype(F32), oth[at_c, :].astype(F32))
        return ab[rows(at_a), :], ab[rows(at_b), :].astype(F32), tc

    def two(s):
        (ta0, tb0, tc0), (ta1, tb1, tc1) = tiles(s), tiles(s + 1)
        none = jnp.zeros((T, R), BF)
        ta = jnp.concatenate(
            [jnp.concatenate([ta0, none], axis=1), jnp.concatenate([none, ta1], axis=1)], axis=0
        )
        tb = jnp.concatenate([tb0, tb1], axis=1)
        tc = jnp.concatenate([tc0, tc1], axis=1)
        pair = (tb[:, None, :] * tc[None, :, :]).reshape(T * T, 2 * R).astype(BF)
        model = lax.dot_general(ta, pair, (((1,), (1,)), ((), ())), preferred_element_type=F32)
        resids = []
        for u in range(2):
            live = (s + u < count).astype(F32).astype(BF)
            part = model[u * T : (u + 1) * T, :] - obs_v[s + u].astype(F32)
            resids.append(live * part.astype(BF))
            res_v[s + u] = resids[u]
        resid = jnp.concatenate(resids, axis=0)
        term_a = jnp.dot(resid, pair, preferred_element_type=F32)
        wide = lax.dot_general(resid, ta, (((0,), (0,)), ((), ())), preferred_element_type=F32)
        wide = wide.reshape(T, T, 2 * R)
        term_b = jnp.sum(wide * tc[None, :, :], axis=1)
        term_c = jnp.sum(wide * tb[:, None, :], axis=0)
        return [
            (term_a[u * T : (u + 1) * T, u * R : (u + 1) * R],
             term_b[:, u * R : (u + 1) * R], term_c[:, u * R : (u + 1) * R])
            for u in range(2)
        ]

    def group(g, carry):
        base = g * UNROLL
        load(g).wait()

        @pl.when(base < count)
        def _():
            found = [t for u in range(0, UNROLL, 2) for t in two(base + u)]
            for u, (term_a, term_b, term_c) in enumerate(found):
                at_a, at_b, y, in_plane, other = places(base + u)
                acc_ab[rows(at_a), :] += term_a
                acc_ab[rows(at_b), :] += term_b
                acc[rows(other * 2048 + y * 512 + in_plane), :] += term_c

        @pl.when(base >= count)
        def _():
            res_v[pl.ds(base, UNROLL)] = jnp.zeros((UNROLL,) + res.shape[1:], BF)

        store(g).start()
        return carry

    lax.fori_loop(0, groups, group, 0)
    out_ab[...] = acc_ab[...].astype(BF)
    out_own[...] = acc[:2048, :]
    out_oth[...] = acc[2048:, :].astype(BF)
    for g in range(groups):
        store(g).wait()


def run_kernel(pos, counts, ab, own, oth, obs):
    slots = obs.shape[0]
    groups = slots // UNROLL
    return pl.pallas_call(
        cp_kernel,
        out_shape=(jax.ShapeDtypeStruct(obs.shape, BF),
                   sds(4 * AB), sds(2048, F32), sds(2048)),
        in_specs=[SMEM, SMEM, VMEM, VMEM, VMEM, HBM],
        out_specs=(HBM, VMEM, VMEM, VMEM),
        scratch_shapes=[
            pltpu.VMEM((4 * AB, R), F32),
            pltpu.VMEM((4096, R), F32),
            pltpu.VMEM(obs.shape, BF),
            pltpu.VMEM(obs.shape, BF),
            pltpu.SemaphoreType.DMA((groups,)),
            pltpu.SemaphoreType.DMA((groups,)),
        ],
        compiler_params=pltpu.CompilerParams(vmem_limit_bytes=48 * 1024 * 1024),
        cost_estimate=pl.CostEstimate(
            flops=slots * 8 * T * T * T * R, bytes_accessed=12_000_000, transcendentals=0
        ),
    )(pos, counts, ab, own, oth, obs)


def on_device(factor_a, factor_b, factor_c, observed, coords, counts):
    slots = observed.shape[3]
    fa, fb, fc = factor_a[0], factor_b[0], factor_c[0]
    swap = [(0, 1), (1, 0)]

    send = spread(fa, fb, fc)
    b_own = fetch(fb)
    got = lax.all_to_all(send, ("zh", "zl"), 0, 0, tiled=True)
    y_send, b_z = small(split_kernel, (sds((4, CY)), sds(128)), got, b_own)
    by_y = lax.all_to_all(y_send, "y", 0, 0, tiled=True)
    b_oth = lax.ppermute(b_z, "co", swap)
    x_send = small(join_kernel, sds(AB), by_y, b_z, b_oth)
    by_y, x_send = lax.optimization_barrier((by_y, x_send))
    by_x = lax.all_gather(x_send, "x", axis=0)
    c_oth = lax.ppermute(by_y, "co", swap)

    res, sum_ab, sum_own, sum_oth = run_kernel(
        coords.reshape(3, slots),
        counts.reshape(1),
        by_x.reshape(4 * AB, R),
        by_y.reshape(4 * CY, R),
        c_oth.reshape(4 * CY, R),
        observed[0, 0, 0],
    )

    ab_in = lax.all_to_all(sum_ab.reshape(4, AB, R), "x", 0, 0, tiled=True)
    c_in = lax.ppermute(sum_oth, "co", swap)
    y_send, b_own, b_send = small(
        pack_y_kernel, (sds((4, CY)), sds(128, F32), sds(128)), ab_in, sum_own, c_in
    )
    ca_in = lax.all_to_all(y_send, "y", 0, 0, tiled=True)
    b_in = lax.ppermute(b_send, "co", swap)
    send, b_keep = small(
        pack_z_kernel, (sds((16, 2 * T)), sds(T, F32)), ca_in, b_own, b_in
    )
    got = lax.all_to_all(send, ("zh", "zl"), 0, 0, tiled=True)
    grad_a, grad_b, grad_c = small(last_kernel, (sds(T, F32),) * 3, got, b_keep)
    return (res.reshape(observed.shape), grad_a[None], grad_b[None], grad_c[None])


def solution(mesh):
    fine = Mesh(mesh.devices.reshape(4, 2, 4, 4, 4), ("zl", "co", "zh", "y", "x"))
    ia, ja = ("zl", "co"), ("zh", "y")
    return jax.shard_map(
        on_device,
        mesh=fine,
        in_specs=(
            P(ia, (*ja, "x"), None),
            P(ja, (*ia, "x"), None),
            P("x", (*ia, *ja), None),
            P(ia, ja, "x", None, None, None),
            P(None, ia, ja, "x", None),
            P(ia, ja, "x"),
        ),
        out_specs=(
            P(ia, ja, "x", None, None, None),
            P(ia, (*ja, "x"), None),
            P(ja, (*ia, "x"), None),
            P("x", (*ia, *ja), None),
        ),
        check_vma=False,
    )
```

```python
import jax
import jax.numpy as jnp
from jax import lax
from jax.experimental import pallas as pl
from jax.experimental.pallas import tpu as pltpu
from jax.sharding import Mesh, PartitionSpec as P

BF = jnp.bfloat16
F32 = jnp.float32
T = 32
R = 128
CHUNK = 12
VMEM = pl.BlockSpec(memory_space=pltpu.VMEM)
SMEM = pl.BlockSpec(memory_space=pltpu.SMEM)
HBM = pl.BlockSpec(memory_space=pltpu.HBM)

AB = 768
CY = 640


def sds(rows, dtype=BF):
    return jax.ShapeDtypeStruct(rows + (R,) if isinstance(rows, tuple) else (rows, R), dtype)


def small(kernel, out_shape, *args):
    return pl.pallas_call(
        kernel,
        out_shape=out_shape,
        in_specs=[VMEM] * len(args),
        out_specs=jax.tree.map(lambda _: VMEM, out_shape),
        compiler_params=pltpu.CompilerParams(vmem_limit_bytes=8 * 1024 * 1024),
    )(*args)


def spread_kernel(fa, fb, fc, send, a_v, b_v, c_v, sem):
    zl = lax.axis_index("zl")
    copies = [
        pltpu.make_async_copy(src, dst, sem.at[n])
        for n, (src, dst) in enumerate(((fa, a_v), (fb, b_v), (fc, c_v)))
    ]
    for copy in copies:
        copy.start()
    for copy in copies:
        copy.wait()
    for i in range(4):
        second = jnp.where(zl == i, a_v[...], b_v[...])
        for j in range(4):
            send[4 * j + i, :T, :] = c_v[...]
            send[4 * j + i, T:, :] = second


def spread(fa, fb, fc):
    return pl.pallas_call(
        spread_kernel,
        out_shape=sds((16, 2 * T)),
        in_specs=[HBM, HBM, HBM],
        out_specs=VMEM,
        scratch_shapes=[pltpu.VMEM((T, R), BF)] * 3 + [pltpu.SemaphoreType.DMA((3,))],
        compiler_params=pltpu.CompilerParams(vmem_limit_bytes=60 * 1024 * 1024),
    )(fa, fb, fc)


def fetch_kernel(fb, b_own, sem):
    copy = pltpu.make_async_copy(fb, b_own, sem)
    copy.start()
    copy.wait()


def fetch(fb):
    return pl.pallas_call(
        fetch_kernel,
        out_shape=sds(T),
        in_specs=[HBM],
        out_specs=VMEM,
        scratch_shapes=[pltpu.SemaphoreType.DMA],
        compiler_params=pltpu.CompilerParams(vmem_limit_bytes=8 * 1024 * 1024),
        cost_estimate=pl.CostEstimate(flops=0, bytes_accessed=1_000_000, transcendentals=0),
    )(fb)


def split_kernel(got, b_own, y_send, b_z):
    zl, zh = lax.axis_index("zl"), lax.axis_index("zh")
    for m in range(16):
        tile = got[m, :T, :]
        for k in range(4):
            y_send[k, m * T : (m + 1) * T, :] = tile
    for j in range(4):
        tile = got[4 * j + zl, T:, :]
        for k in range(4):
            y_send[k, 512 + j * T : 512 + (j + 1) * T, :] = tile
    for i in range(4):
        b_z[i * T : (i + 1) * T, :] = jnp.where(zl == i, b_own[...], got[4 * zh + i, T:, :])


def join_kernel(by_y, b_z, b_oth, x_send):
    for j in range(4):
        x_send[128 * j : 128 * (j + 1), :] = by_y[j, 512:, :]
    x_send[512:640, :] = b_z[...]
    x_send[640:, :] = b_oth[...]


def total(ref, rows):
    parts = [ref[k, rows, :].astype(F32) for k in range(4)]
    return (parts[0] + parts[1]) + (parts[2] + parts[3])


def pack_y_kernel(ab_in, own, c_in, y_send, b_own, b_oth):
    for k in range(4):
        rows = slice(512 * k, 512 * (k + 1))
        y_send[k, :512, :] = (own[rows, :] + c_in[rows, :].astype(F32)).astype(BF)
        y_send[k, 512:, :] = total(ab_in, slice(128 * k, 128 * (k + 1))).astype(BF)
    b_own[...] = total(ab_in, slice(512, 640))
    b_oth[...] = total(ab_in, slice(640, 768)).astype(BF)


def pack_z_kernel(ca_in, b_own, b_in, send, b_keep):
    zl = lax.axis_index("zl")
    for m in range(16):
        send[m, :T, :] = total(ca_in, slice(m * T, (m + 1) * T)).astype(BF)
    a = [total(ca_in, slice(512 + j * T, 512 + (j + 1) * T)) for j in range(4)]
    for i in range(4):
        rows = slice(i * T, (i + 1) * T)
        b = b_own[rows, :] + b_in[rows, :].astype(F32)
        for j in range(4):
            send[4 * j + i, T:, :] = jnp.where(zl == i, a[j], b).astype(BF)

        @pl.when(zl == i)
        def _():
            b_keep[...] = b


def last_kernel(got, b_keep, grad_a, grad_b, grad_c):
    zl, zh = lax.axis_index("zl"), lax.axis_index("zh")
    scale = 1.0 / T
    c = got[0, :T, :].astype(F32)
    for m in range(1, 16):
        c = c + got[m, :T, :].astype(F32)
    grad_c[...] = c * scale
    a = got[zl, T:, :].astype(F32)
    for j in range(1, 4):
        a = a + got[4 * j + zl, T:, :].astype(F32)
    grad_a[...] = a * scale
    b = b_keep[...]
    for i in range(4):
        b = b + jnp.where(zl == i, 0.0, got[4 * zh + i, T:, :].astype(F32))
    grad_b[...] = b * scale


def cp_kernel(pos, counts, ab, own, oth, obs, res, out_ab, out_own, out_oth,
              acc_ab, acc, obs_v, res_v, in_sem, out_sem):
    slots = obs.shape[0]
    chunks = slots // CHUNK
    co = lax.axis_index("co")
    count = counts[0]

    def load(g):
        part = pl.ds(g * CHUNK, CHUNK)
        return pltpu.make_async_copy(obs.at[part], obs_v.at[part], in_sem.at[g])

    def store(g):
        part = pl.ds(g * CHUNK, CHUNK)
        return pltpu.make_async_copy(res_v.at[part], res.at[part], out_sem.at[g])

    for g in range(chunks):
        load(g).start()
    acc_ab[...] = jnp.zeros_like(acc_ab)
    acc[...] = jnp.zeros_like(acc)

    def rows(start):
        return pl.ds(pl.multiple_of(start, T), T)

    def places(s):
        pa, pb, pc = pos[0, s], pos[1, s], pos[2, s]
        at_a = (pa & 3) * AB + ((pa >> 2) & 3) * 128 + (pa >> 4) * T
        at_b = (pb & 3) * AB + 512 + (((pb >> 2) & 1) ^ co) * 128 + (pb >> 3) * T
        in_plane = (((pc >> 2) & 3) * 4 + (pc >> 5)) * T
        return at_a, at_b, pc & 3, in_plane, ((pc >> 4) & 1) ^ co

    def tiles(s):
        at_a, at_b, y, in_plane, other = places(s)
        at_c = rows(y * CY + in_plane)
        tc = jnp.where(other == 0, own[at_c, :].astype(F32), oth[at_c, :].astype(F32))
        return ab[rows(at_a), :], ab[rows(at_b), :].astype(F32), tc

    def two(s):
        (ta0, tb0, tc0), (ta1, tb1, tc1) = tiles(s), tiles(s + 1)
        none = jnp.zeros((T, R), BF)
        ta = jnp.concatenate(
            [jnp.concatenate([ta0, none], axis=1), jnp.concatenate([none, ta1], axis=1)], axis=0
        )
        tb = jnp.concatenate([tb0, tb1], axis=1)
        tc = jnp.concatenate([tc0, tc1], axis=1)
        pair = (tb[:, None, :] * tc[None, :, :]).reshape(T * T, 2 * R).astype(BF)
        model = lax.dot_general(ta, pair, (((1,), (1,)), ((), ())), preferred_element_type=F32)
        resids = []
        for u in range(2):
            live = (s + u < count).astype(F32).astype(BF)
            part = model[u * T : (u + 1) * T, :] - obs_v[s + u].astype(F32)
            resids.append(live * part.astype(BF))
            res_v[s + u] = resids[u]
        resid = jnp.concatenate(resids, axis=0)
        term_a = jnp.dot(resid, pair, preferred_element_type=F32)
        wide = lax.dot_general(resid, ta, (((0,), (0,)), ((), ())), preferred_element_type=F32)
        wide = wide.reshape(T, T, 2 * R)
        term_b = jnp.sum(wide * tc[None, :, :], axis=1)
        term_c = jnp.sum(wide * tb[:, None, :], axis=0)
        return [
            (term_a[u * T : (u + 1) * T, u * R : (u + 1) * R],
             term_b[:, u * R : (u + 1) * R], term_c[:, u * R : (u + 1) * R])
            for u in range(2)
        ]

    found = []
    for g in range(chunks):
        load(g).wait()
    for g in range(chunks):
        for u in range(0, CHUNK, 2):
            found += two(g * CHUNK + u)
        store(g).start()
    for s, (term_a, term_b, term_c) in enumerate(found):
        at_a, at_b, y, in_plane, other = places(s)
        acc_ab[rows(at_a), :] += term_a
        acc_ab[rows(at_b), :] += term_b
        acc[rows(other * 2048 + y * 512 + in_plane), :] += term_c

    out_ab[...] = acc_ab[...].astype(BF)
    out_own[...] = acc[:2048, :]
    out_oth[...] = acc[2048:, :].astype(BF)
    for g in range(chunks):
        store(g).wait()


def run_kernel(pos, counts, ab, own, oth, obs):
    slots = obs.shape[0]
    chunks = slots // CHUNK
    return pl.pallas_call(
        cp_kernel,
        out_shape=(jax.ShapeDtypeStruct(obs.shape, BF),
                   sds(4 * AB), sds(2048, F32), sds(2048)),
        in_specs=[SMEM, SMEM, VMEM, VMEM, VMEM, HBM],
        out_specs=(HBM, VMEM, VMEM, VMEM),
        scratch_shapes=[
            pltpu.VMEM((4 * AB, R), F32),
            pltpu.VMEM((4096, R), F32),
            pltpu.VMEM(obs.shape, BF),
            pltpu.VMEM(obs.shape, BF),
            pltpu.SemaphoreType.DMA((chunks,)),
            pltpu.SemaphoreType.DMA((chunks,)),
        ],
        compiler_params=pltpu.CompilerParams(vmem_limit_bytes=48 * 1024 * 1024),
        cost_estimate=pl.CostEstimate(
            flops=slots * 8 * T * T * T * R, bytes_accessed=12_000_000, transcendentals=0
        ),
    )(pos, counts, ab, own, oth, obs)


def on_device(factor_a, factor_b, factor_c, observed, coords, counts):
    slots = observed.shape[3]
    fa, fb, fc = factor_a[0], factor_b[0], factor_c[0]
    swap = [(0, 1), (1, 0)]

    send = spread(fa, fb, fc)
    b_own = fetch(fb)
    got = lax.all_to_all(send, ("zh", "zl"), 0, 0, tiled=True)
    y_send, b_z = small(split_kernel, (sds((4, CY)), sds(128)), got, b_own)
    by_y = lax.all_to_all(y_send, "y", 0, 0, tiled=True)
    b_oth = lax.ppermute(b_z, "co", swap)
    x_send = small(join_kernel, sds(AB), by_y, b_z, b_oth)
    by_y, x_send = lax.optimization_barrier((by_y, x_send))
    by_x = lax.all_gather(x_send, "x", axis=0)
    c_oth = lax.ppermute(by_y, "co", swap)

    res, sum_ab, sum_own, sum_oth = run_kernel(
        coords.reshape(3, slots),
        counts.reshape(1),
        by_x.reshape(4 * AB, R),
        by_y.reshape(4 * CY, R),
        c_oth.reshape(4 * CY, R),
        observed[0, 0, 0],
    )

    ab_in = lax.all_to_all(sum_ab.reshape(4, AB, R), "x", 0, 0, tiled=True)
    c_in = lax.ppermute(sum_oth, "co", swap)
    y_send, b_own, b_send = small(
        pack_y_kernel, (sds((4, CY)), sds(128, F32), sds(128)), ab_in, sum_own, c_in
    )
    ca_in = lax.all_to_all(y_send, "y", 0, 0, tiled=True)
    b_in = lax.ppermute(b_send, "co", swap)
    send, b_keep = small(
        pack_z_kernel, (sds((16, 2 * T)), sds(T, F32)), ca_in, b_own, b_in
    )
    got = lax.all_to_all(send, ("zh", "zl"), 0, 0, tiled=True)
    grad_a, grad_b, grad_c = small(last_kernel, (sds(T, F32),) * 3, got, b_keep)
    return (res.reshape(observed.shape), grad_a[None], grad_b[None], grad_c[None])


def solution(mesh):
    fine = Mesh(mesh.devices.reshape(4, 2, 4, 4, 4), ("zl", "co", "zh", "y", "x"))
    ia, ja = ("zl", "co"), ("zh", "y")
    return jax.shard_map(
        on_device,
        mesh=fine,
        in_specs=(
            P(ia, (*ja, "x"), None),
            P(ja, (*ia, "x"), None),
            P("x", (*ia, *ja), None),
            P(ia, ja, "x", None, None, None),
            P(None, ia, ja, "x", None),
            P(ia, ja, "x"),
        ),
        out_specs=(
            P(ia, ja, "x", None, None, None),
            P(ia, (*ja, "x"), None),
            P(ja, (*ia, "x"), None),
            P("x", (*ia, *ja), None),
        ),
        check_vma=False,
    )
```
